32 devices in a mesh: pool: 8 (over y, x, core), tp: 4 (over z).
Axes of the slice: x: 2, y: 2, z: 4, core: 2. Of those that a mesh axis runs over, the one named last changes fastest.
Arguments:
- projected_mixer: bfloat16 [256, 4, 8192], P('pool', None, 'tp'), may hold values from -6 to 6
- projected_gate: bfloat16 [256, 4, 8192], P('pool', None, 'tp'), may hold values from -6 to 6
- slot_state_cache: bfloat16 [512, 19, 8192], P('pool', None, 'tp'), may hold values from -6 to 6
- session_holder: int32 [256], P('pool'), may hold values from 0 to 7, as said below
- session_slot: int32 [256], P('pool'), may hold values from 0 to 63, as said below
- conversation_customer: int32 [256], P('pool'), may hold values from 0 to 63
- filter_tap_weight: float32 [4, 8192], P(None, 'tp'), may hold values from -3 to 3
- filter_bias: float32 [8192], P('tp'), may hold values from -3 to 3
- lowrank_step_weight: bfloat16 [8192, 512], P('tp'), may hold values from -0.0625 to 0.0625
- state_maps_weight: bfloat16 [8192, 32], P('tp'), may hold values from -0.0625 to 0.0625
- adapter_down_maps: bfloat16 [8192, 1024], P('tp'), may hold values from -0.0625 to 0.0625
- adapter_up_maps: bfloat16 [1024, 512], replicated, may hold values from -1.5 to 1.5
- step_size_gain: float32 [512], replicated, may hold values from 0.5 to 1.5
- step_up_weight: bfloat16 [512, 8192], P(None, 'tp'), may hold values from -0.25 to 0.25
- step_size_bias: float32 [8192], P('tp'), may hold values from -4 to -1
- log_decay_rates: float32 [16, 8192], P(None, 'tp'), may hold values from 0 to 2.77
- skip_factor: float32 [8192], P('tp'), may hold values from 0.5 to 1.5
Outputs:
- gated_out: bfloat16 [256, 4, 8192], P('pool', None, 'tp')
- new_cache: bfloat16 [512, 19, 8192], P('pool', None, 'tp')
The draws below stay inside these ranges and needn't reach their ends.
Inputs may be any that keep to these rules, and one draw needn't show every extreme that they name: `session_holder`: within the 32 rows of one index of pool, no owner is named by more than 8 rows. `session_slot`: no two rows name the same owner and slot.
All inputs are finite; a program needn't handle non-finite values.
Results may differ from the reference program's by a relative error of at most 0.0055.
Values may be sent and summed in bfloat16 or wider, within the bound.
A program may use at most 128 MiB of HBM per device.

```python
import math
import jax
import jax.numpy as jnp
import numpy as np
from jax import lax

INNER_WIDTH = 8192
STATE = 16
CONV = 4
STEP_SIZE_RANK = 512
ADAPTER_RANK = 16
TENANT_COUNT = 64
STEPS = 4
R_DEV = 32
CAP = 8
ROWS = 256
POOL_DEV = 64
POOL = 512
N_POOL = 8


def choose_rows(key):
    heat_key, base_key, order_key, slot_key = jax.random.split(key, 4)
    eligible_entries = N_POOL * CAP
    heat_rank = jax.random.permutation(heat_key, N_POOL)
    recency_degree = jnp.maximum(3 - heat_rank, 0)
    recency_reward = recency_degree * 2 ** 19
    keeper_table = jnp.arange(eligible_entries) // CAP
    bare_merit = jax.random.randint(base_key, (N_POOL, eligible_entries), 0, 2 ** 20)
    combined_merits = (bare_merit + recency_reward[keeper_table][None, :]) * eligible_entries + (eligible_entries - 1 - jnp.arange(eligible_entries))[None, :]
    chosen_idx = jnp.argsort(-combined_merits, axis=1)[:, :R_DEV]
    shuffle_score = jax.random.randint(order_key, (N_POOL, R_DEV), 0, 2 ** 20) * R_DEV + jnp.arange(R_DEV)[None, :]
    shuffle_idx = jnp.argsort(shuffle_score, axis=1)
    chosen_idx = jnp.take_along_axis(chosen_idx, shuffle_idx, axis=1)
    owner_idx = chosen_idx // CAP
    copy_idx = chosen_idx % CAP
    block_idx = jnp.arange(N_POOL)[:, None]
    slot_score = jax.random.randint(slot_key, (N_POOL, POOL_DEV), 0, 2 ** 20) * POOL_DEV + jnp.arange(POOL_DEV)[None, :]
    slot_perm = jnp.argsort(slot_score, axis=1)
    slot_idx = slot_perm[owner_idx, block_idx * CAP + copy_idx]
    return (owner_idx.reshape(-1).astype(jnp.int32), slot_idx.reshape(-1).astype(jnp.int32))


def draw_session_holder(key, part):
    owner_idx, slot_idx = choose_rows(key)
    return owner_idx


def draw_session_slot(key, part):
    owner_idx, slot_idx = choose_rows(key)
    return slot_idx


def place_ends(values, rng, smallest, high):
    shape = values.shape
    spot = [jax.random.randint(jax.random.fold_in(rng, axis), (), 0, shape[axis]) for axis in range(len(shape))]
    values = values.at[tuple(spot)].set(smallest)
    longest = shape.index(max(shape))
    spot[longest] = (spot[longest] + 1) % shape[longest]
    return values.at[tuple(spot)].set(high)


def levels(key, extent, cuts, smallest, largest):
    def one(position, blocks):
        steps = jax.random.uniform(jax.random.fold_in(jax.random.fold_in(key, 6), position), (blocks,), jnp.float32, smallest / len(cuts), largest / len(cuts))
        return jnp.repeat(jnp.exp(steps), extent[position] // blocks).reshape((-1,) + (1,) * (len(extent) - position - 1))

    gain = one(*cuts[0])
    for cut in cuts[1:]:
        gain = gain * one(*cut)
    return gain


def rank_table(count, skew):
    portions = [(1 << 20) // math.isqrt(rank ** skew) + 1 for rank in range(1, count + 1)]
    spread = 1 + sum(portions) // (1 << 30)
    return np.cumsum(np.array([max(1, weight // spread) for weight in portions]))


def skewed_ids(own_key, extent, number_of, slope):
    grid = rank_table(number_of, slope)
    pick = jax.random.randint(jax.random.fold_in(own_key, 1), extent, 0, int(grid[number_of - 1]))
    standing = jnp.searchsorted(jnp.asarray(grid, jnp.int32), pick, side="right")
    return jax.random.permutation(jax.random.fold_in(own_key, 2), number_of)[standing].astype(jnp.int32)


def centred(stream_key, extent, scale, reach, cuts=(), held_as=jnp.bfloat16):
    drawn = jax.random.normal(stream_key, extent, jnp.float32) * scale
    if len(cuts) > 0:
        drawn = levels(stream_key, extent, cuts, -0.22, 0.18) * drawn
    return jnp.clip(drawn, min=-reach, max=reach).astype(held_as)


def setup_inputs(seed: int = 0) -> dict:
    keys = jax.random.split(jax.random.key(seed), 18)
    return {
        "projected_mixer": centred(keys[0], (ROWS, STEPS, INNER_WIDTH), 1.0, 6.0, ((0, 8), (2, 4))),
        "projected_gate": centred(keys[1], (ROWS, STEPS, INNER_WIDTH), 1.0, 6.0, ((0, 8), (2, 4))),
        "slot_state_cache": centred(keys[2], (POOL, STATE + CONV - 1, INNER_WIDTH), 1.0, 6.0, ((0, 8), (2, 4))),
        "session_holder": draw_session_holder(jax.random.fold_in(keys[17], 71), 0),
        "session_slot": draw_session_slot(jax.random.fold_in(keys[17], 71), 0),
        "conversation_customer": place_ends(skewed_ids(keys[5], (ROWS,), TENANT_COUNT, 2), jax.random.fold_in(keys[5], 3), 0, TENANT_COUNT - 1).astype(jnp.int32),
        "filter_tap_weight": centred(keys[6], (CONV, INNER_WIDTH), CONV ** -0.5, 3.0, ((1, 4),), jnp.float32),
        "filter_bias": centred(keys[7], (INNER_WIDTH,), 0.5, 3.0, ((0, 4),), jnp.float32),
        "lowrank_step_weight": centred(keys[8], (INNER_WIDTH, STEP_SIZE_RANK), INNER_WIDTH ** -0.5, 0.0625, ((0, 4),)),
        "state_maps_weight": centred(keys[9], (INNER_WIDTH, 2 * STATE), INNER_WIDTH ** -0.5, 0.0625, ((0, 4),)),
        "adapter_down_maps": centred(keys[10], (INNER_WIDTH, TENANT_COUNT * ADAPTER_RANK), INNER_WIDTH ** -0.5, 0.0625, ((0, 4),)),
        "adapter_up_maps": centred(keys[11], (TENANT_COUNT * ADAPTER_RANK, STEP_SIZE_RANK), ADAPTER_RANK ** -0.5, 1.5),
        "step_size_gain": jnp.clip(1.0 + 0.1 * jax.random.normal(keys[12], (STEP_SIZE_RANK,), jnp.float32), 0.5, 1.5),
        "step_up_weight": centred(keys[13], (STEP_SIZE_RANK, INNER_WIDTH), STEP_SIZE_RANK ** -0.5, 0.25, ((1, 4),)),
        "step_size_bias": jnp.clip(-4.0 + 3.0 * jax.random.uniform(keys[14], (INNER_WIDTH,), jnp.float32) ** levels(keys[14], (INNER_WIDTH,), ((0, 4),), -0.2, 0.2), -4.0, -1.0),
        "log_decay_rates": jnp.clip(2.77 * jax.random.uniform(keys[15], (STATE, INNER_WIDTH), jnp.float32) ** levels(keys[15], (STATE, INNER_WIDTH), ((1, 4),), -0.2, 0.2), 0.0, 2.77),
        "skip_factor": jnp.clip(0.5 + 1.0 * jax.random.uniform(keys[16], (INNER_WIDTH,), jnp.float32) ** levels(keys[16], (INNER_WIDTH,), ((0, 4),), -0.2, 0.2), 0.5, 1.5),
    }


def mixer_rows(mixer_inputs, switch_arguments, saved_state, tenant_list, filter_tap_weight, filter_bias, lowrank_step_weight, state_maps_weight, adapter_down_maps, adapter_up_maps, step_size_gain, step_up_weight, step_size_bias, log_decay_rates, skip_factor):
    row_count, step_count, chan_count = mixer_inputs.shape
    window = jnp.concatenate([saved_state[:, STATE:, :], mixer_inputs], axis=1)
    conv_sum = filter_bias[None, None, :] + jnp.zeros((row_count, step_count, chan_count), jnp.float32)
    for tap_idx in range(filter_tap_weight.shape[0]):
        conv_sum = conv_sum + filter_tap_weight[tap_idx][None, None, :] * window[:, tap_idx:tap_idx + step_count, :].astype(jnp.float32)
    activated = jax.nn.silu(conv_sum).astype(jnp.bfloat16)
    flattened_rows = activated.reshape(row_count * step_count, chan_count)
    lowrank_sum = jnp.dot(flattened_rows, lowrank_step_weight, preferred_element_type=jnp.float32)
    mapped = jnp.dot(flattened_rows, state_maps_weight, preferred_element_type=jnp.float32)
    every_adapter = jnp.dot(flattened_rows, adapter_down_maps, preferred_element_type=jnp.float32)
    tenant_flat = jnp.repeat(tenant_list, step_count)
    selected_rows = jnp.arange(TENANT_COUNT, dtype=jnp.int32)[None, :] == tenant_flat[:, None]
    adapter_applied = lax.optimization_barrier(jnp.sum(jnp.where(selected_rows[:, :, None], every_adapter.reshape(-1, TENANT_COUNT, ADAPTER_RANK), 0.0), axis=1))
    adapter_middle = jnp.where(selected_rows[:, :, None], adapter_applied[:, None, :], 0.0).reshape(-1, TENANT_COUNT * ADAPTER_RANK).astype(jnp.bfloat16)
    adapter_term = jnp.dot(adapter_middle, adapter_up_maps, preferred_element_type=jnp.float32)
    before_norm = lowrank_sum + adapter_term
    mean_sq = lax.optimization_barrier(jnp.mean(before_norm * before_norm, axis=1, keepdims=True))
    normed = (before_norm / jnp.sqrt(mean_sq + 1e-06) * step_size_gain[None, :]).astype(jnp.bfloat16)
    delta = jax.nn.softplus(jnp.dot(normed, step_up_weight, preferred_element_type=jnp.float32) + step_size_bias[None, :])
    delta = delta.reshape(row_count, step_count, chan_count)
    maps_in = mapped[:, :STATE].reshape(row_count, step_count, STATE)
    maps_out = mapped[:, STATE:].reshape(row_count, step_count, STATE)
    decay_base = -jnp.exp(log_decay_rates)
    act_wide = activated.astype(jnp.float32)
    state_now = saved_state[:, :STATE, :].astype(jnp.float32)
    collected = []
    for step_idx in range(step_count):
        decay_rate = jnp.exp(delta[:, step_idx, None, :] * decay_base[None, :, :])
        driven = (delta[:, step_idx, :] * act_wide[:, step_idx, :])[:, None, :] * maps_in[:, step_idx, :, None]
        state_now = decay_rate * state_now + driven
        output_now = lax.optimization_barrier(jnp.sum(maps_out[:, step_idx, :, None] * state_now, axis=1)) + skip_factor[None, :] * act_wide[:, step_idx, :]
        output_now = output_now * jax.nn.silu(switch_arguments[:, step_idx, :].astype(jnp.float32))
        collected.append(output_now)
    gated_result = jnp.stack(collected, axis=1).astype(jnp.bfloat16)
    newest_state = jnp.concatenate([state_now.astype(jnp.bfloat16), window[:, step_count:, :]], axis=1)
    return (gated_result, newest_state)

def reference(projected_mixer, projected_gate, slot_state_cache, session_holder, session_slot, conversation_customer, filter_tap_weight, filter_bias, lowrank_step_weight, state_maps_weight, adapter_down_maps, adapter_up_maps, step_size_gain, step_up_weight, step_size_bias, log_decay_rates, skip_factor):
    global_slot = (session_holder * POOL_DEV + session_slot).astype(jnp.int32)
    saved_state = slot_state_cache[global_slot]
    gated_result, newest_state = mixer_rows(projected_mixer, projected_gate, saved_state, conversation_customer, filter_tap_weight, filter_bias, lowrank_step_weight, state_maps_weight, adapter_down_maps, adapter_up_maps, step_size_gain, step_up_weight, step_size_bias, log_decay_rates, skip_factor)
    return (gated_result, slot_state_cache.at[global_slot].set(newest_state))
```

```python
import jax
import jax.numpy as jnp
from jax import lax
from jax.sharding import PartitionSpec as P

STATE = 16
ADAPTER_RANK = 16
TENANT_COUNT = 64


def one_hot_rows(index_list, count):
    return (index_list[:, None] == jnp.arange(count, dtype=jnp.int32)[None, :]).astype(jnp.bfloat16)


def take_rows(table, index_list):
    flattened = table.reshape(table.shape[0], -1)
    selector = one_hot_rows(index_list, table.shape[0])
    picked = jnp.dot(selector, flattened, preferred_element_type=jnp.float32).astype(table.dtype)
    return picked.reshape((index_list.shape[0],) + table.shape[1:])


def place_rows(values, index_list, count):
    flattened = values.reshape(values.shape[0], -1)
    selector = one_hot_rows(index_list, count)
    placed = jnp.dot(selector.T, flattened, preferred_element_type=jnp.float32).astype(values.dtype)
    return placed.reshape((count,) + values.shape[1:])


def mixer_rows(
    mixer_inputs,
    switch_arguments,
    saved_state,
    tenant_list,
    filter_tap_weight,
    filter_bias,
    lowrank_step_weight,
    state_maps_weight,
    adapter_down_maps,
    adapter_up_maps,
    step_size_gain,
    step_up_weight,
    step_size_bias,
    log_decay_rates,
    skip_factor,
):
    row_count, step_count, chan_count = mixer_inputs.shape
    window = jnp.concatenate([saved_state[:, STATE:, :], mixer_inputs], axis=1)
    conv_sum = filter_bias[None, None, :] + jnp.zeros(
        (row_count, step_count, chan_count), jnp.float32
    )
    for tap_idx in range(filter_tap_weight.shape[0]):
        conv_sum = conv_sum + filter_tap_weight[tap_idx][None, None, :] * window[
            :, tap_idx : tap_idx + step_count, :
        ].astype(jnp.float32)
    activated = jax.nn.silu(conv_sum).astype(jnp.bfloat16)
    flattened_rows = activated.reshape(row_count * step_count, chan_count)
    part_low = jnp.dot(flattened_rows, lowrank_step_weight, preferred_element_type=jnp.float32)
    part_maps = jnp.dot(flattened_rows, state_maps_weight, preferred_element_type=jnp.float32)
    every_adapter = jnp.dot(flattened_rows, adapter_down_maps, preferred_element_type=jnp.float32)
    tenant_flat = jnp.repeat(tenant_list, step_count)
    selected_rows = jnp.arange(TENANT_COUNT, dtype=jnp.int32)[None, :] == tenant_flat[:, None]
    part_adapt = jnp.sum(
        jnp.where(
            selected_rows[:, :, None], every_adapter.reshape(-1, TENANT_COUNT, ADAPTER_RANK), 0.0
        ),
        axis=1,
    )
    lowrank_sum, mapped, adapter_applied = lax.psum((part_low, part_maps, part_adapt), "tp")
    adapter_middle = (
        jnp.where(selected_rows[:, :, None], adapter_applied[:, None, :], 0.0)
        .reshape(-1, TENANT_COUNT * ADAPTER_RANK)
        .astype(jnp.bfloat16)
    )
    adapter_term = jnp.dot(adapter_middle, adapter_up_maps, preferred_element_type=jnp.float32)
    before_norm = lowrank_sum + adapter_term
    mean_sq = jnp.mean(before_norm * before_norm, axis=1, keepdims=True)
    normed = (before_norm / jnp.sqrt(mean_sq + 1e-06) * step_size_gain[None, :]).astype(
        jnp.bfloat16
    )
    delta = jax.nn.softplus(
        jnp.dot(normed, step_up_weight, preferred_element_type=jnp.float32)
        + step_size_bias[None, :]
    )
    delta = delta.reshape(row_count, step_count, chan_count)
    maps_in = mapped[:, :STATE].reshape(row_count, step_count, STATE)
    maps_out = mapped[:, STATE:].reshape(row_count, step_count, STATE)
    decay_base = -jnp.exp(log_decay_rates)
    act_wide = activated.astype(jnp.float32)
    state_now = saved_state[:, :STATE, :].astype(jnp.float32)
    collected = []
    for step_idx in range(step_count):
        decay_rate = jnp.exp(delta[:, step_idx, None, :] * decay_base[None, :, :])
        driven = (delta[:, step_idx, :] * act_wide[:, step_idx, :])[:, None, :] * maps_in[
            :, step_idx, :, None
        ]
        state_now = decay_rate * state_now + driven
        output_now = (
            jnp.sum(maps_out[:, step_idx, :, None] * state_now, axis=1)
            + skip_factor[None, :] * act_wide[:, step_idx, :]
        )
        output_now = output_now * jax.nn.silu(switch_arguments[:, step_idx, :].astype(jnp.float32))
        collected.append(output_now)
    gated_result = jnp.stack(collected, axis=1).astype(jnp.bfloat16)
    newest_state = jnp.concatenate(
        [state_now.astype(jnp.bfloat16), window[:, step_count:, :]], axis=1
    )
    return (gated_result, newest_state)


def local(
    projected_mixer,
    projected_gate,
    slot_state_cache,
    session_holder,
    session_slot,
    conversation_customer,
    *weights,
):
    owners = lax.axis_size("pool")
    slot_count, depth_rows, chan_count = slot_state_cache.shape
    row_count, step_count, _ = projected_mixer.shape
    per_owner = slot_count // owners
    owner_match = (session_holder[:, None] == jnp.arange(owners, dtype=jnp.int32)[None, :]).astype(
        jnp.int32
    )
    owner_rank = jnp.sum((jnp.cumsum(owner_match, axis=0) - 1) * owner_match, axis=1)
    target = session_holder * per_owner + owner_rank

    def exchange(values):
        return lax.all_to_all(
            values.reshape((owners, per_owner) + values.shape[1:]),
            "pool",
            split_axis=0,
            concat_axis=0,
            tiled=True,
        ).reshape(values.shape)

    labels = jnp.concatenate(
        [
            one_hot_rows(session_slot, slot_count),
            one_hot_rows(conversation_customer, TENANT_COUNT),
        ],
        axis=1,
    )
    labels = jnp.broadcast_to(labels[:, None, :], (row_count, step_count, labels.shape[1]))
    sent = place_rows(jnp.concatenate([projected_mixer, labels], axis=2), target, slot_count)
    sent_gate = place_rows(projected_gate, target, slot_count)
    arrived = exchange(sent)
    arrived_gate = exchange(sent_gate)
    selector = arrived[:, 0, chan_count : chan_count + slot_count]

    def to_slots(values):
        flattened = values.reshape(slot_count, -1)
        return (
            jnp.dot(selector.T, flattened, preferred_element_type=jnp.float32)
            .astype(jnp.bfloat16)
            .reshape(values.shape)
        )

    tenant_mask = to_slots(arrived[:, 0, chan_count + slot_count :])
    tenant_list = jnp.argmax(tenant_mask, axis=1).astype(jnp.int32)
    reached = jnp.sum(selector, axis=0) > 0
    gated_slots, newest_state = mixer_rows(
        to_slots(arrived[:, :, :chan_count]),
        to_slots(arrived_gate),
        slot_state_cache,
        tenant_list,
        *weights,
    )
    new_cache = jnp.where(reached[:, None, None], newest_state, slot_state_cache)
    returned = jnp.dot(
        selector, gated_slots.reshape(slot_count, -1), preferred_element_type=jnp.float32
    ).astype(jnp.bfloat16)
    came_back = exchange(returned.reshape(gated_slots.shape))
    gated_result = take_rows(came_back, target)
    return (gated_result, new_cache)


def solution(mesh):
    placed = (
        P("pool", None, "tp"),
        P("pool", None, "tp"),
        P("pool", None, "tp"),
        P("pool"),
        P("pool"),
        P("pool"),
        P(None, "tp"),
        P("tp"),
        P("tp", None),
        P("tp", None),
        P("tp", None),
        P(),
        P(),
        P(None, "tp"),
        P("tp"),
        P(None, "tp"),
        P("tp"),
    )
    return jax.shard_map(
        local,
        mesh=mesh,
        in_specs=placed,
        out_specs=(P("pool", None, "tp"), P("pool", None, "tp")),
        check_vma=False,
    )
```

```python
import functools

import jax
import jax.numpy as jnp
from jax import lax
from jax.experimental import pallas as pl
from jax.experimental.pallas import tpu as pltpu
from jax.sharding import PartitionSpec as P

STATE = 16
ADAPTER_RANK = 16
TENANT_COUNT = 64
LABELS = 128
VMEM_BYTES = 50 * 1024 * 1024
F32 = jnp.float32
BF16 = jnp.bfloat16


def iota(shape, dim):
    return lax.broadcasted_iota(jnp.int32, shape, dim)


def as_bf16(mask):
    return jnp.where(mask, 1.0, 0.0).astype(BF16)


def whole_vmem():
    return pl.BlockSpec(memory_space=pltpu.VMEM)


def whole_any():
    return pl.BlockSpec(memory_space=pl.ANY)


def fixed(shape):
    return pl.BlockSpec(shape, lambda c: (0,) * len(shape))


def dispatch_matrix(holder, owners, per_owner, steps):
    lanes = holder.shape[1]
    named = jnp.where(iota((owners, lanes), 0) == holder, 1.0, 0.0)
    earlier = as_bf16(
        (iota((lanes, lanes), 0) // steps < iota((lanes, lanes), 1) // steps)
        & (iota((lanes, lanes), 0) % steps == 0)
    )
    before = jnp.dot(named.astype(BF16), earlier, preferred_element_type=F32)
    rank = jnp.sum(named * before, axis=0, keepdims=True)
    target = holder.astype(F32) * per_owner + rank
    shape = (owners * per_owner * steps, lanes)
    return jnp.where(
        ((iota(shape, 0) // steps).astype(F32) == target)
        & (iota(shape, 0) % steps == iota(shape, 1) % steps),
        1.0,
        0.0,
    )


def greet(pool_count, tp_count):
    barrier = pltpu.get_barrier_semaphore()
    me, mine = lax.axis_index("pool"), lax.axis_index("tp")
    for k in range(1, pool_count):
        pl.semaphore_signal(
            barrier,
            inc=1,
            device_id={"pool": lax.rem(me + k, pool_count)},
            device_id_type=pl.DeviceIdType.MESH,
        )
    for k in range(1, tp_count):
        pl.semaphore_signal(
            barrier,
            inc=1,
            device_id={"tp": lax.rem(mine + k, tp_count)},
            device_id_type=pl.DeviceIdType.MESH,
        )
    pl.semaphore_wait(barrier, max(pool_count - 1, 0) + max(tp_count - 1, 0))


def spread(source, landing, send_sem, recv_sem, local_sem, axis, count):
    me = lax.axis_index(axis)
    copies = []
    for k in range(1, count):
        there = lax.rem(me + k, count)
        copy = pltpu.make_async_remote_copy(
            src_ref=source.at[there],
            dst_ref=landing.at[me],
            send_sem=send_sem.at[k],
            recv_sem=recv_sem.at[k],
            device_id={axis: there},
            device_id_type=pl.DeviceIdType.MESH,
        )
        copy.start()
        copies.append(copy)
    own = pltpu.make_async_copy(source.at[me], landing.at[me], local_sem)
    own.start()
    copies.append(own)
    return copies


def pick_rows(selector, rows_ref, out_ref, offset=0):
    owners, block, _ = out_ref.shape
    for at in range(0, rows_ref.shape[1], 512):
        wide = min(512, rows_ref.shape[1] - at)
        part = jnp.dot(selector, rows_ref[:, at : at + wide], preferred_element_type=F32)
        out_ref[:, :, at : at + wide] = part.reshape(owners, block, wide).astype(BF16)


def send_rows(
    owners,
    per_owner,
    steps,
    holder_ref,
    slot_ref,
    tenant_ref,
    rows_ref,
    arrived_ref,
    back_ref,
    outgoing,
    send_sem,
    recv_sem,
    local_sem,
):
    picked = dispatch_matrix(holder_ref[...], owners, per_owner, steps)
    selector = picked.astype(BF16)
    back_ref[...] = picked.T.astype(BF16)
    lanes = rows_ref.shape[0]
    chans = rows_ref.shape[1]
    slots = owners * per_owner
    column = iota((lanes, LABELS), 1)
    labels = as_bf16((column == slot_ref[...]) | (column == tenant_ref[...] + slots))
    marked = jnp.dot(selector, labels, preferred_element_type=F32)
    outgoing[:, :, chans:] = marked.reshape(owners, per_owner * steps, LABELS).astype(BF16)
    pick_rows(selector, rows_ref, outgoing)
    greet(owners, 1)
    for copy in spread(outgoing, arrived_ref, send_sem, recv_sem, local_sem, "pool", owners):
        copy.wait()


def project(
    steps,
    tp_count,
    arrived_ref,
    label_ref,
    conv_ref,
    tap_ref,
    bias_ref,
    low_ref,
    maps_ref,
    down_ref,
    part_ref,
    slots_ref,
    act_ref,
    to_arrival_ref,
    to_slot_ref,
    mask_ref,
    low_acc,
    maps_acc,
    down_acc,
):
    chunk = pl.program_id(0)
    slots = conv_ref.shape[1]
    total = slots * steps
    wide = act_ref.shape[1]

    @pl.when(chunk == 0)
    def _():
        labels = label_ref[...].astype(F32).reshape(total, LABELS)
        lane = iota((LABELS, total), 0)
        expand = as_bf16(lane == iota((LABELS, total), 1) % slots)
        selected = jnp.dot(labels.astype(BF16), expand, preferred_element_type=F32)
        selected = jnp.where(
            iota((total, total), 0) % steps == iota((total, total), 1) // slots, selected, 0.0
        )
        to_arrival_ref[...] = selected.astype(BF16)
        turned = selected.T.astype(BF16)
        to_slot_ref[...] = turned
        mask_ref[...] = jnp.dot(
            turned, labels.astype(BF16), preferred_element_type=F32
        ).astype(BF16)
        low_acc[...] = jnp.zeros_like(low_acc)
        maps_acc[...] = jnp.zeros_like(maps_acc)
        down_acc[...] = jnp.zeros_like(down_acc)

    rows = arrived_ref[...].astype(F32).reshape(total, wide).astype(BF16)
    mixed = jnp.dot(to_slot_ref[...], rows, preferred_element_type=F32)
    slots_ref[...] = mixed.astype(BF16)
    window = [conv_ref[k].astype(F32) for k in range(conv_ref.shape[0])]
    window += [mixed[s * slots : (s + 1) * slots] for s in range(steps)]
    for s in range(steps):
        summed = jnp.broadcast_to(bias_ref[...], (slots, wide))
        for k in range(tap_ref.shape[0]):
            summed = summed + tap_ref[k : k + 1, :] * window[s + k]
        act_ref[s * slots : (s + 1) * slots, :] = (summed / (1.0 + jnp.exp(-summed))).astype(BF16)
    act = act_ref[...]
    low_acc[...] += jnp.dot(act, low_ref[...], preferred_element_type=F32)
    maps_acc[...] += jnp.dot(act, maps_ref[...], preferred_element_type=F32)
    down_acc[...] += jnp.dot(act, down_ref[...], preferred_element_type=F32)

    @pl.when(chunk == pl.num_programs(0) - 1)
    def _():
        ranks = down_acc.shape[1]
        column = iota((LABELS, ranks), 1) // ADAPTER_RANK
        keep = jnp.dot(
            mask_ref[...],
            as_bf16(iota((LABELS, ranks), 0) == column + slots),
            preferred_element_type=F32,
        )
        chosen = down_acc[...] * keep
        folded = chosen[:, :LABELS]
        for at in range(LABELS, ranks, LABELS):
            folded = folded + chosen[:, at : at + LABELS]
        fold = as_bf16(
            iota((LABELS, LABELS), 1)
            == iota((LABELS, LABELS), 0) % ADAPTER_RANK + 2 * STATE
        )
        tail = maps_acc[...] + jnp.dot(folded.astype(BF16), fold, preferred_element_type=F32)
        rank = low_acc.shape[1]
        part_ref[:, :, :rank] = (
            low_acc[...].reshape(tp_count, total // tp_count, rank).astype(BF16)
        )
        part_ref[:, :, rank:] = tail.reshape(tp_count, total // tp_count, LABELS).astype(BF16)


def join(
    owners,
    per_owner,
    steps,
    tp_count,
    holder_ref,
    gate_ref,
    part_ref,
    mask_ref,
    up_ref,
    gain_ref,
    arrived_ref,
    normed_ref,
    tail_ref,
    outgoing,
    landed,
    normed_own,
    tail_own,
    gate_send,
    gate_recv,
    gate_local,
    part_send,
    part_recv,
    normed_send,
    normed_recv,
    tail_send,
    tail_recv,
    own_sem,
):
    mine = lax.axis_index("tp")
    greet(owners, tp_count)
    first = []
    for k in range(1, tp_count):
        there = lax.rem(mine + k, tp_count)
        copy = pltpu.make_async_remote_copy(
            src_ref=part_ref.at[there],
            dst_ref=landed.at[k - 1],
            send_sem=part_send.at[k],
            recv_sem=part_recv.at[k],
            device_id={"tp": there},
            device_id_type=pl.DeviceIdType.MESH,
        )
        copy.start()
        first.append(copy)
    selector = dispatch_matrix(holder_ref[...], owners, per_owner, steps).astype(BF16)
    pick_rows(selector, gate_ref, outgoing)
    gates = spread(outgoing, arrived_ref, gate_send, gate_recv, gate_local, "pool", owners)
    summed = part_ref[mine].astype(F32)
    for k in range(1, tp_count):
        first[k - 1].wait()
        summed = summed + landed[k - 1].astype(F32)
    rank = gain_ref.shape[1]
    low, tail = summed[:, :rank], summed[:, rank:]
    ranks = up_ref.shape[0]
    slots = owners * per_owner
    column = iota((LABELS, ranks), 1)
    lane = iota((LABELS, ranks), 0)
    repeated = jnp.dot(
        tail.astype(BF16),
        as_bf16(lane == column % ADAPTER_RANK + 2 * STATE),
        preferred_element_type=F32,
    )
    keep = jnp.dot(
        mask_ref[mine],
        as_bf16(lane == column // ADAPTER_RANK + slots),
        preferred_element_type=F32,
    )
    middle = (repeated * keep).astype(BF16)
    pre = low + jnp.dot(middle, up_ref[...], preferred_element_type=F32)
    mean_sq = jnp.mean(pre * pre, axis=1, keepdims=True)
    normed_own[...] = (pre / jnp.sqrt(mean_sq + 1e-06) * gain_ref[...]).astype(BF16)
    tail_own[...] = tail
    last = []
    for number, (own, landing, send_sem, recv_sem) in enumerate(
        (
            (normed_own, normed_ref, normed_send, normed_recv),
            (tail_own, tail_ref, tail_send, tail_recv),
        )
    ):
        for k in range(1, tp_count):
            copy = pltpu.make_async_remote_copy(
                src_ref=own,
                dst_ref=landing.at[mine],
                send_sem=send_sem.at[k],
                recv_sem=recv_sem.at[k],
                device_id={"tp": lax.rem(mine + k, tp_count)},
                device_id_type=pl.DeviceIdType.MESH,
            )
            copy.start()
            last.append(copy)
        kept = pltpu.make_async_copy(own, landing.at[mine], own_sem.at[number])
        kept.start()
        last.append(kept)
    for copy in last + gates:
        copy.wait()


def scan(
    steps,
    normed_ref,
    tail_ref,
    up_ref,
    bias_ref,
    rate_ref,
    skip_ref,
    act_ref,
    slots_ref,
    gate_ref,
    to_arrival_ref,
    to_slot_ref,
    cache_ref,
    new_ref,
    out_ref,
    maps,
    delta,
    driven,
    newest,
    result,
    reached,
    decay,
):
    slots = cache_ref.shape[0]
    total = slots * steps
    wide = act_ref.shape[1]

    @pl.when(pl.program_id(0) == 0)
    def _():
        turned = tail_ref[...].T
        for at in range(total):
            maps[at] = jnp.broadcast_to(turned[: 2 * STATE, at : at + 1], (2 * STATE, LABELS))
        found = jnp.sum(to_slot_ref[:slots, :].astype(F32), axis=1, keepdims=True)
        reached[...] = jnp.broadcast_to(found, (slots, wide))

    drawn = jnp.dot(normed_ref[...], up_ref[...], preferred_element_type=F32) + bias_ref[...]
    size = jnp.maximum(drawn, 0.0) + jnp.log1p(jnp.exp(-jnp.abs(drawn)))
    act = act_ref[...].astype(F32)
    delta[...] = size
    driven[...] = size * act
    newest[...] = slots_ref[...].astype(F32)
    decay[...] = -jnp.exp(rate_ref[...])
    copies = wide // LABELS

    def one(slot, carry):
        base = decay[...]
        old = cache_ref[slot, :STATE, :].astype(F32)
        state = old
        for s in range(steps):
            at = s * slots + slot
            row = delta[pl.ds(at, 1), :]
            push = driven[pl.ds(at, 1), :]
            maps_in = jnp.concatenate([maps[at, :STATE, :]] * copies, axis=1)
            maps_out = jnp.concatenate([maps[at, STATE:, :]] * copies, axis=1)
            state = jnp.exp(row * base) * state + push * maps_in
            result[pl.ds(at, 1), :] = jnp.sum(maps_out * state, axis=0, keepdims=True)
        served = reached[pl.ds(slot, 1), :] > 0.5
        new_ref[slot, :STATE, :] = jnp.where(served, state, old).astype(BF16)
        kept = cache_ref[slot, STATE:, :].astype(F32)
        taken = jnp.concatenate(
            [newest[pl.ds(s * slots + slot, 1), :] for s in range(1, steps)], axis=0
        )
        new_ref[slot, STATE:, :] = jnp.where(served, taken, kept).astype(BF16)
        return carry

    lax.fori_loop(0, slots, one, 0)
    rows = gate_ref[...].astype(F32).reshape(total, wide).astype(BF16)
    gate = jnp.dot(to_slot_ref[...], rows, preferred_element_type=F32)
    gated = (result[...] + skip_ref[...] * act) * (gate / (1.0 + jnp.exp(-gate)))
    back = jnp.dot(to_arrival_ref[...], gated.astype(BF16), preferred_element_type=F32)
    out_ref[...] = back.reshape(out_ref.shape).astype(BF16)


def return_rows(owners, back_ref, result_ref, out_ref, landed, send_sem, recv_sem, local_sem):
    greet(owners, 1)
    for copy in spread(result_ref, landed, send_sem, recv_sem, local_sem, "pool", owners):
        copy.wait()
    total = back_ref.shape[1]
    for at in range(0, out_ref.shape[1], 512):
        rows = landed[:, :, at : at + 512].astype(F32).reshape(total, 512).astype(BF16)
        out_ref[:, at : at + 512] = jnp.dot(
            back_ref[...], rows, preferred_element_type=F32
        ).astype(BF16)


def local(
    projected_mixer,
    projected_gate,
    slot_state_cache,
    session_holder,
    session_slot,
    conversation_customer,
    filter_tap_weight,
    filter_bias,
    lowrank_step_weight,
    state_maps_weight,
    adapter_down_maps,
    adapter_up_maps,
    step_size_gain,
    step_up_weight,
    step_size_bias,
    log_decay_rates,
    skip_factor,
):
    owners, tp_count = lax.axis_size("pool"), lax.axis_size("tp")
    slots, depth, chans = slot_state_cache.shape
    served, steps, _ = projected_mixer.shape
    per_owner = slots // owners
    block = per_owner * steps
    total = slots * steps
    share = total // tp_count
    lanes = served * steps
    rank = lowrank_step_weight.shape[1]
    ranks = adapter_down_maps.shape[1]
    dma = pltpu.SemaphoreType.DMA
    shape = jax.ShapeDtypeStruct

    holder = jnp.repeat(session_holder, steps).reshape(1, lanes)
    slot = jnp.repeat(session_slot, steps).reshape(lanes, 1)
    tenant = jnp.repeat(conversation_customer, steps).reshape(lanes, 1)
    mixer = projected_mixer.reshape(lanes, chans)
    gate = projected_gate.reshape(lanes, chans)
    conv = jnp.swapaxes(slot_state_cache[:, STATE:, :], 0, 1)
    maps_weight = jnp.pad(state_maps_weight, ((0, 0), (0, LABELS - 2 * STATE)))

    arrived, back = pl.pallas_call(
        functools.partial(send_rows, owners, per_owner, steps),
        out_shape=(
            shape((owners, block, chans + LABELS), BF16),
            shape((lanes, total), BF16),
        ),
        in_specs=[whole_vmem()] * 4,
        out_specs=(whole_any(), whole_vmem()),
        scratch_shapes=[
            pltpu.VMEM((owners, block, chans + LABELS), BF16),
            dma((owners,)),
            dma((owners,)),
            dma,
        ],
        compiler_params=pltpu.CompilerParams(
            collective_id=0, has_side_effects=True, vmem_limit_bytes=VMEM_BYTES
        ),
        name="send_rows",
    )(holder, slot, tenant, mixer)

    wide = min(512, chans)
    part, by_slot, act, to_arrival, to_slot, mask = pl.pallas_call(
        functools.partial(project, steps, tp_count),
        grid=(chans // wide,),
        out_shape=(
            shape((tp_count, share, rank + LABELS), BF16),
            shape((total, chans), BF16),
            shape((total, chans), BF16),
            shape((total, total), BF16),
            shape((total, total), BF16),
            shape((total, LABELS), BF16),
        ),
        in_specs=[
            pl.BlockSpec((owners, block, wide), lambda c: (0, 0, c)),
            pl.BlockSpec((owners, block, LABELS), lambda c: (0, 0, chans // LABELS)),
            pl.BlockSpec((conv.shape[0], slots, wide), lambda c: (0, 0, c)),
            pl.BlockSpec((filter_tap_weight.shape[0], wide), lambda c: (0, c)),
            pl.BlockSpec((1, wide), lambda c: (0, c)),
            pl.BlockSpec((wide, rank), lambda c: (c, 0)),
            pl.BlockSpec((wide, LABELS), lambda c: (c, 0)),
            pl.BlockSpec((wide, ranks), lambda c: (c, 0)),
        ],
        out_specs=(
            fixed((tp_count, share, rank + LABELS)),
            pl.BlockSpec((total, wide), lambda c: (0, c)),
            pl.BlockSpec((total, wide), lambda c: (0, c)),
            fixed((total, total)),
            fixed((total, total)),
            fixed((total, LABELS)),
        ),
        scratch_shapes=[
            pltpu.VMEM((total, rank), F32),
            pltpu.VMEM((total, LABELS), F32),
            pltpu.VMEM((total, ranks), F32),
        ],
        compiler_params=pltpu.CompilerParams(vmem_limit_bytes=VMEM_BYTES),
        name="project",
    )(
        arrived,
        arrived,
        conv,
        filter_tap_weight,
        filter_bias.reshape(1, chans),
        lowrank_step_weight,
        maps_weight,
        adapter_down_maps,
    )

    arrived_gate, normed, tail = pl.pallas_call(
        functools.partial(join, owners, per_owner, steps, tp_count),
        out_shape=(
            shape((owners, block, chans), BF16),
            shape((tp_count, share, rank), BF16),
            shape((tp_count, share, LABELS), F32),
        ),
        in_specs=[whole_vmem()] * 6,
        out_specs=(whole_any(), whole_any(), whole_any()),
        scratch_shapes=[
            pltpu.VMEM((owners, block, chans), BF16),
            pltpu.VMEM((tp_count - 1, share, rank + LABELS), BF16),
            pltpu.VMEM((share, rank), BF16),
            pltpu.VMEM((share, LABELS), F32),
            dma((owners,)),
            dma((owners,)),
            dma,
            dma((tp_count,)),
            dma((tp_count,)),
            dma((tp_count,)),
            dma((tp_count,)),
            dma((tp_count,)),
            dma((tp_count,)),
            dma((2,)),
        ],
        compiler_params=pltpu.CompilerParams(
            collective_id=1, has_side_effects=True, vmem_limit_bytes=VMEM_BYTES
        ),
        name="join",
    )(
        holder,
        gate,
        part,
        mask.reshape(tp_count, share, LABELS),
        adapter_up_maps,
        step_size_gain.reshape(1, rank),
    )

    new_cache, result = pl.pallas_call(
        functools.partial(scan, steps),
        grid=(chans // wide,),
        out_shape=(
            shape((slots, depth, chans), BF16),
            shape((owners, block, chans), BF16),
        ),
        in_specs=[
            fixed((total, rank)),
            fixed((total, LABELS)),
            pl.BlockSpec((rank, wide), lambda c: (0, c)),
            pl.BlockSpec((1, wide), lambda c: (0, c)),
            pl.BlockSpec((STATE, wide), lambda c: (0, c)),
            pl.BlockSpec((1, wide), lambda c: (0, c)),
            pl.BlockSpec((total, wide), lambda c: (0, c)),
            pl.BlockSpec((total, wide), lambda c: (0, c)),
            pl.BlockSpec((owners, block, wide), lambda c: (0, 0, c)),
            fixed((total, total)),
            fixed((total, total)),
            pl.BlockSpec((slots, depth, wide), lambda c: (0, 0, c)),
        ],
        out_specs=(
            pl.BlockSpec((slots, depth, wide), lambda c: (0, 0, c)),
            pl.BlockSpec((owners, block, wide), lambda c: (0, 0, c)),
        ),
        scratch_shapes=[
            pltpu.VMEM((total, 2 * STATE, LABELS), F32),
            pltpu.VMEM((total, wide), F32),
            pltpu.VMEM((total, wide), F32),
            pltpu.VMEM((total, wide), F32),
            pltpu.VMEM((total, wide), F32),
            pltpu.VMEM((slots, wide), F32),
            pltpu.VMEM((STATE, wide), F32),
        ],
        compiler_params=pltpu.CompilerParams(vmem_limit_bytes=VMEM_BYTES),
        name="scan",
    )(
        normed.reshape(total, rank),
        tail.reshape(total, LABELS),
        step_up_weight,
        step_size_bias.reshape(1, chans),
        log_decay_rates,
        skip_factor.reshape(1, chans),
        act,
        by_slot,
        arrived_gate,
        to_arrival,
        to_slot,
        slot_state_cache,
    )

    gated = pl.pallas_call(
        functools.partial(return_rows, owners),
        out_shape=shape((lanes, chans), BF16),
        in_specs=[whole_vmem()] * 2,
        out_specs=whole_vmem(),
        scratch_shapes=[
            pltpu.VMEM((owners, block, chans), BF16),
            dma((owners,)),
            dma((owners,)),
            dma,
        ],
        compiler_params=pltpu.CompilerParams(
            collective_id=2, has_side_effects=True, vmem_limit_bytes=VMEM_BYTES
        ),
        name="return_rows",
    )(back, result)
    return (gated.reshape(served, steps, chans), new_cache)


def solution(mesh):
    placed = (
        P("pool", None, "tp"),
        P("pool", None, "tp"),
        P("pool", None, "tp"),
        P("pool"),
        P("pool"),
        P("pool"),
        P(None, "tp"),
        P("tp"),
        P("tp", None),
        P("tp", None),
        P("tp", None),
        P(),
        P(),
        P(None, "tp"),
        P("tp"),
        P(None, "tp"),
        P("tp"),
    )
    return jax.shard_map(
        local,
        mesh=mesh,
        in_specs=placed,
        out_specs=(P("pool", None, "tp"), P("pool", None, "tp")),
        check_vma=False,
    )
```

```python
import functools

import jax
import jax.numpy as jnp
from jax import lax
from jax.experimental import pallas as pl
from jax.experimental.pallas import tpu as pltpu
from jax.sharding import PartitionSpec as P

STATE = 16
ADAPTER_RANK = 16
TENANT_COUNT = 64
LABELS = 128
VMEM_BYTES = 50 * 1024 * 1024
LOG2_E = 1.4426950408889634
F32 = jnp.float32
BF16 = jnp.bfloat16


def iota(shape, dim):
    return lax.broadcasted_iota(jnp.int32, shape, dim)


def as_bf16(mask):
    return jnp.where(mask, 1.0, 0.0).astype(BF16)


def whole_vmem():
    return pl.BlockSpec(memory_space=pltpu.VMEM)


def whole_any():
    return pl.BlockSpec(memory_space=pl.ANY)


def fixed(shape):
    return pl.BlockSpec(shape, lambda c: (0,) * len(shape))


def per_lane(numbers, steps):
    rows = numbers.shape[1]
    shape = (rows, rows * steps)
    wide = as_bf16(iota(shape, 0) == iota(shape, 1) // steps)
    return jnp.dot(numbers.astype(F32).astype(BF16), wide, preferred_element_type=F32)


def dispatch_matrix(holder, owners, per_owner, steps):
    lanes = holder.shape[1] * steps
    holder = per_lane(holder, steps)
    named = jnp.where(iota((owners, lanes), 0).astype(F32) == holder, 1.0, 0.0)
    earlier = as_bf16(
        (iota((lanes, lanes), 0) // steps < iota((lanes, lanes), 1) // steps)
        & (iota((lanes, lanes), 0) % steps == 0)
    )
    before = jnp.dot(named.astype(BF16), earlier, preferred_element_type=F32)
    rank = jnp.sum(named * before, axis=0, keepdims=True)
    target = holder * per_owner + rank
    shape = (owners * per_owner * steps, lanes)
    return jnp.where(
        ((iota(shape, 0) // steps).astype(F32) == target)
        & (iota(shape, 0) % steps == iota(shape, 1) % steps),
        1.0,
        0.0,
    )


def greet(pool_count, tp_count):
    announce(pool_count, tp_count)
    await_all(pool_count, tp_count)


def await_all(pool_count, tp_count):
    pl.semaphore_wait(
        pltpu.get_barrier_semaphore(), max(pool_count - 1, 0) + max(tp_count - 1, 0)
    )


def announce(pool_count, tp_count):
    barrier = pltpu.get_barrier_semaphore()
    me, mine = lax.axis_index("pool"), lax.axis_index("tp")
    for k in range(1, pool_count):
        pl.semaphore_signal(
            barrier,
            inc=1,
            device_id={"pool": lax.rem(me + k, pool_count)},
            device_id_type=pl.DeviceIdType.MESH,
        )
    for k in range(1, tp_count):
        pl.semaphore_signal(
            barrier,
            inc=1,
            device_id={"tp": lax.rem(mine + k, tp_count)},
            device_id_type=pl.DeviceIdType.MESH,
        )


def spread(source, landing, send_sem, recv_sem, local_sem, axis, count):
    me = lax.axis_index(axis)
    copies = []
    for k in range(1, count):
        there = lax.rem(me + k, count)
        copy = pltpu.make_async_remote_copy(
            src_ref=source.at[there],
            dst_ref=landing.at[me],
            send_sem=send_sem.at[k],
            recv_sem=recv_sem.at[k],
            device_id={axis: there},
            device_id_type=pl.DeviceIdType.MESH,
        )
        copy.start()
        copies.append(copy)
    own = pltpu.make_async_copy(source.at[me], landing.at[me], local_sem)
    own.start()
    copies.append(own)
    return copies


def pick_rows(selector, rows_ref, out_ref, offset=0):
    owners, block, _ = out_ref.shape
    for at in range(0, rows_ref.shape[1], 512):
        wide = min(512, rows_ref.shape[1] - at)
        part = jnp.dot(selector, rows_ref[:, at : at + wide], preferred_element_type=F32)
        out_ref[:, :, at : at + wide] = part.reshape(owners, block, wide).astype(BF16)


def send_rows(
    owners,
    per_owner,
    steps,
    holder_ref,
    slot_ref,
    tenant_ref,
    rows_ref,
    arrived_ref,
    back_ref,
    outgoing,
    send_sem,
    recv_sem,
    local_sem,
):
    announce(owners, 1)
    picked = dispatch_matrix(holder_ref[...], owners, per_owner, steps)
    selector = picked.astype(BF16)
    back_ref[...] = picked.T.astype(BF16)
    lanes = rows_ref.shape[0]
    chans = rows_ref.shape[1]
    slots = owners * per_owner
    line = iota((LABELS, lanes), 0).astype(F32)
    labels = as_bf16(
        (line == per_lane(slot_ref[...], steps))
        | (line == per_lane(tenant_ref[...], steps) + slots)
    )
    marked = lax.dot_general(
        selector, labels, (((1,), (1,)), ((), ())), preferred_element_type=F32
    )
    outgoing[:, :, chans:] = marked.reshape(owners, per_owner * steps, LABELS).astype(BF16)
    pick_rows(selector, rows_ref, outgoing)
    await_all(owners, 1)
    for copy in spread(outgoing, arrived_ref, send_sem, recv_sem, local_sem, "pool", owners):
        copy.wait()


def project(
    steps,
    tp_count,
    arrived_ref,
    conv_ref0,
    conv_ref1,
    conv_ref2,
    tap_ref,
    bias_ref,
    low_ref,
    maps_ref,
    down_ref,
    part_ref,
    slots_ref,
    act_ref,
    to_arrival_ref,
    to_slot_ref,
    mask_ref,
    low_acc,
    maps_acc,
    down_acc,
):
    chunk = pl.program_id(0)
    slots, wide = conv_ref0.shape[1:]
    total = slots * steps
    chans = arrived_ref.shape[2] - LABELS

    @pl.when(chunk == 0)
    def _():
        labels = arrived_ref[:, :, chans:].astype(F32).reshape(total, LABELS)
        lane = iota((LABELS, total), 0)
        expand = as_bf16(lane == iota((LABELS, total), 1) % slots)
        selected = jnp.dot(labels.astype(BF16), expand, preferred_element_type=F32)
        selected = jnp.where(
            iota((total, total), 0) % steps == iota((total, total), 1) // slots, selected, 0.0
        )
        to_arrival_ref[...] = selected.astype(BF16)
        turned = selected.T.astype(BF16)
        to_slot_ref[...] = turned
        mask_ref[...] = jnp.dot(
            turned, labels.astype(BF16), preferred_element_type=F32
        ).astype(BF16)
        low_acc[...] = jnp.zeros_like(low_acc)
        maps_acc[...] = jnp.zeros_like(maps_acc)
        down_acc[...] = jnp.zeros_like(down_acc)

    columns = pl.ds(pl.multiple_of(chunk * wide, wide), wide)
    rows = arrived_ref[:, :, columns].astype(F32).reshape(total, wide).astype(BF16)
    mixed = jnp.dot(to_slot_ref[...], rows, preferred_element_type=F32)
    slots_ref[...] = mixed.astype(BF16)
    window = [conv_ref[0].astype(F32) for conv_ref in (conv_ref0, conv_ref1, conv_ref2)]
    window += [mixed[s * slots : (s + 1) * slots] for s in range(steps)]
    for s in range(steps):
        summed = jnp.broadcast_to(bias_ref[...], (slots, wide))
        for k in range(tap_ref.shape[0]):
            summed = summed + tap_ref[k : k + 1, :] * window[s + k]
        act_ref[s * slots : (s + 1) * slots, :] = (summed / (1.0 + jnp.exp(-summed))).astype(BF16)
    act = act_ref[...]
    low_acc[...] += jnp.dot(act, low_ref[...], preferred_element_type=F32)
    maps_acc[:, : 2 * STATE] += lax.dot_general(
        act, maps_ref[...], (((1,), (1,)), ((), ())), preferred_element_type=F32
    )
    down_acc[...] += jnp.dot(act, down_ref[...], preferred_element_type=F32)

    @pl.when(chunk == pl.num_programs(0) - 1)
    def _():
        ranks = down_acc.shape[1]
        column = iota((LABELS, ranks), 1) // ADAPTER_RANK
        keep = jnp.dot(
            mask_ref[...],
            as_bf16(iota((LABELS, ranks), 0) == column + slots),
            preferred_element_type=F32,
        )
        chosen = down_acc[...] * keep
        folded = chosen[:, :LABELS]
        for at in range(LABELS, ranks, LABELS):
            folded = folded + chosen[:, at : at + LABELS]
        fold = as_bf16(
            iota((LABELS, LABELS), 1)
            == iota((LABELS, LABELS), 0) % ADAPTER_RANK + 2 * STATE
        )
        tail = maps_acc[...] + jnp.dot(folded.astype(BF16), fold, preferred_element_type=F32)
        rank = low_acc.shape[1]
        part_ref[:, :, :rank] = (
            low_acc[...].reshape(tp_count, total // tp_count, rank).astype(BF16)
        )
        part_ref[:, :, rank:] = tail.reshape(tp_count, total // tp_count, LABELS).astype(BF16)


def join(
    owners,
    per_owner,
    steps,
    tp_count,
    holder_ref,
    gate_ref,
    part_ref,
    mask_ref,
    up_ref,
    gain_ref,
    arrived_ref,
    normed_ref,
    tail_ref,
    outgoing,
    landed,
    normed_own,
    tail_own,
    gate_send,
    gate_recv,
    gate_local,
    part_send,
    part_recv,
    normed_send,
    normed_recv,
    tail_send,
    tail_recv,
    own_sem,
):
    mine = lax.axis_index("tp")
    greet(owners, tp_count)
    first = []
    for k in range(1, tp_count):
        there = lax.rem(mine + k, tp_count)
        copy = pltpu.make_async_remote_copy(
            src_ref=part_ref.at[there],
            dst_ref=landed.at[k - 1],
            send_sem=part_send.at[k],
            recv_sem=part_recv.at[k],
            device_id={"tp": there},
            device_id_type=pl.DeviceIdType.MESH,
        )
        copy.start()
        first.append(copy)
    selector = dispatch_matrix(holder_ref[...], owners, per_owner, steps).astype(BF16)
    pick_rows(selector, gate_ref, outgoing)
    gates = spread(outgoing, arrived_ref, gate_send, gate_recv, gate_local, "pool", owners)
    summed = part_ref[mine].astype(F32)
    for k in range(1, tp_count):
        first[k - 1].wait()
        summed = summed + landed[k - 1].astype(F32)
    rank = gain_ref.shape[1]
    low, tail = summed[:, :rank], summed[:, rank:]
    ranks = up_ref.shape[0]
    slots = owners * per_owner
    column = iota((LABELS, ranks), 1)
    lane = iota((LABELS, ranks), 0)
    repeated = jnp.dot(
        tail.astype(BF16),
        as_bf16(lane == column % ADAPTER_RANK + 2 * STATE),
        preferred_element_type=F32,
    )
    keep = jnp.dot(
        mask_ref[mine],
        as_bf16(lane == column // ADAPTER_RANK + slots),
        preferred_element_type=F32,
    )
    middle = (repeated * keep).astype(BF16)
    pre = low + jnp.dot(middle, up_ref[...], preferred_element_type=F32)
    mean_sq = jnp.mean(pre * pre, axis=1, keepdims=True)
    normed_own[...] = (pre / jnp.sqrt(mean_sq + 1e-06) * gain_ref[...]).astype(BF16)
    tail_own[...] = tail
    last = []
    for number, (own, landing, send_sem, recv_sem) in enumerate(
        (
            (normed_own, normed_ref, normed_send, normed_recv),
            (tail_own, tail_ref, tail_send, tail_recv),
        )
    ):
        for k in range(1, tp_count):
            copy = pltpu.make_async_remote_copy(
                src_ref=own,
                dst_ref=landing.at[mine],
                send_sem=send_sem.at[k],
                recv_sem=recv_sem.at[k],
                device_id={"tp": lax.rem(mine + k, tp_count)},
                device_id_type=pl.DeviceIdType.MESH,
            )
            copy.start()
            last.append(copy)
        kept = pltpu.make_async_copy(own, landing.at[mine], own_sem.at[number])
        kept.start()
        last.append(kept)
    for copy in last + gates:
        copy.wait()


def scan(
    steps,
    normed_ref,
    tail_ref,
    up_ref,
    bias_ref,
    rate_ref,
    skip_ref,
    act_ref,
    slots_ref,
    gate_ref,
    to_arrival_ref,
    to_slot_ref,
    cache_ref,
    new_ref,
    out_ref,
    maps,
    delta,
    driven,
    result,
    reached,
    decay,
):
    slots, wide = cache_ref.shape[1:]
    total = slots * steps
    group, tile = 16, LABELS
    tiles = wide // tile
    chunk = pl.program_id(0)

    @pl.when(chunk == 0)
    def _():
        for n in range(2 * STATE):
            maps[n] = jnp.broadcast_to(tail_ref[:, n : n + 1], (total, LABELS))
        found = jnp.sum(to_slot_ref[:slots, :].astype(F32), axis=1, keepdims=True)
        reached[...] = jnp.broadcast_to(found, (slots, LABELS))

    drawn = jnp.dot(normed_ref[...], up_ref[...], preferred_element_type=F32) + bias_ref[...]
    size = jnp.maximum(drawn, 0.0) + jnp.log1p(jnp.exp(-jnp.abs(drawn)))
    act = act_ref[...].astype(F32)
    delta[...] = size
    driven[...] = size * act
    decay[...] = jnp.exp(rate_ref[...]) * -LOG2_E

    def one(place, carry):
        first = place // tiles * group
        rows = pl.ds(pl.multiple_of(first, group), group)
        cols = pl.ds(pl.multiple_of(lax.rem(place, tiles) * tile, tile), tile)
        at = [pl.ds(pl.multiple_of(s * slots + first, group), group) for s in range(steps)]
        sizes = [delta[at[s], cols] for s in range(steps)]
        pushes = [driven[at[s], cols] for s in range(steps)]
        served = reached[rows, :] > 0.5
        sums = [jnp.zeros((group, tile), F32)] * steps
        for n in range(STATE):
            old = cache_ref[n, rows, cols].astype(F32)
            base = decay[n : n + 1, cols]
            state = old
            for s in range(steps):
                state = jnp.exp2(sizes[s] * base) * state + pushes[s] * maps[n, at[s], :]
                sums[s] = sums[s] + maps[STATE + n, at[s], :] * state
            new_ref[n, rows, cols] = jnp.where(served, state, old).astype(BF16)
        for s in range(steps):
            result[at[s], cols] = sums[s]
        kept = cache_ref.shape[0] - STATE
        for k in range(kept):
            taken = slots_ref[at[steps - kept + k], cols].astype(F32)
            old = cache_ref[STATE + k, rows, cols].astype(F32)
            new_ref[STATE + k, rows, cols] = jnp.where(served, taken, old).astype(BF16)
        return carry

    lax.fori_loop(0, slots // group * tiles, one, 0)
    columns = pl.ds(pl.multiple_of(chunk * wide, wide), wide)
    rows = gate_ref[:, :, columns].astype(F32).reshape(total, wide).astype(BF16)
    gate = jnp.dot(to_slot_ref[...], rows, preferred_element_type=F32)
    gated = (result[...] + skip_ref[...] * act) * (gate / (1.0 + jnp.exp(-gate)))
    back = jnp.dot(to_arrival_ref[...], gated.astype(BF16), preferred_element_type=F32)
    out_ref[...] = back.reshape(out_ref.shape).astype(BF16)


def return_rows(owners, back_ref, result_ref, out_ref, landed, send_sem, recv_sem, local_sem):
    greet(owners, 1)
    for copy in spread(result_ref, landed, send_sem, recv_sem, local_sem, "pool", owners):
        copy.wait()
    total = back_ref.shape[1]
    for at in range(0, out_ref.shape[1], 512):
        rows = landed[:, :, at : at + 512].astype(F32).reshape(total, 512).astype(BF16)
        out_ref[:, at : at + 512] = jnp.dot(
            back_ref[...], rows, preferred_element_type=F32
        ).astype(BF16)


def local(
    projected_mixer,
    projected_gate,
    slot_state_cache,
    session_holder,
    session_slot,
    conversation_customer,
    filter_tap_weight,
    filter_bias,
    lowrank_step_weight,
    state_maps_weight,
    adapter_down_maps,
    adapter_up_maps,
    step_size_gain,
    step_up_weight,
    step_size_bias,
    log_decay_rates,
    skip_factor,
):
    owners, tp_count = lax.axis_size("pool"), lax.axis_size("tp")
    slots, depth, chans = slot_state_cache.shape
    served, steps, _ = projected_mixer.shape
    per_owner = slots // owners
    block = per_owner * steps
    total = slots * steps
    share = total // tp_count
    lanes = served * steps
    rank = lowrank_step_weight.shape[1]
    ranks = adapter_down_maps.shape[1]
    dma = pltpu.SemaphoreType.DMA
    shape = jax.ShapeDtypeStruct

    holder = session_holder.reshape(1, served)
    slot = session_slot.reshape(1, served)
    tenant = conversation_customer.reshape(1, served)
    mixer = projected_mixer.reshape(lanes, chans)
    gate = projected_gate.reshape(lanes, chans)
    cache = jnp.swapaxes(slot_state_cache, 0, 1)
    maps_weight = state_maps_weight.T

    def conv_row(k):
        return pl.BlockSpec((1, slots, wide), lambda c: (k, 0, c))

    arrived, back = pl.pallas_call(
        functools.partial(send_rows, owners, per_owner, steps),
        out_shape=(
            shape((owners, block, chans + LABELS), BF16),
            shape((lanes, total), BF16),
        ),
        in_specs=[whole_vmem()] * 4,
        out_specs=(whole_any(), whole_vmem()),
        scratch_shapes=[
            pltpu.VMEM((owners, block, chans + LABELS), BF16),
            dma((owners,)),
            dma((owners,)),
            dma,
        ],
        compiler_params=pltpu.CompilerParams(
            collective_id=0, has_side_effects=True, vmem_limit_bytes=VMEM_BYTES
        ),
        name="send_rows",
    )(holder, slot, tenant, mixer)

    wide = min(512, chans)
    part, by_slot, act, to_arrival, to_slot, mask = pl.pallas_call(
        functools.partial(project, steps, tp_count),
        grid=(chans // wide,),
        out_shape=(
            shape((tp_count, share, rank + LABELS), BF16),
            shape((total, chans), BF16),
            shape((total, chans), BF16),
            shape((total, total), BF16),
            shape((total, total), BF16),
            shape((total, LABELS), BF16),
        ),
        in_specs=[
            whole_vmem(),
            conv_row(depth - 3),
            conv_row(depth - 2),
            conv_row(depth - 1),
            pl.BlockSpec((filter_tap_weight.shape[0], wide), lambda c: (0, c)),
            pl.BlockSpec((1, wide), lambda c: (0, c)),
            pl.BlockSpec((wide, rank), lambda c: (c, 0)),
            pl.BlockSpec((2 * STATE, wide), lambda c: (0, c)),
            pl.BlockSpec((wide, ranks), lambda c: (c, 0)),
        ],
        out_specs=(
            fixed((tp_count, share, rank + LABELS)),
            pl.BlockSpec((total, wide), lambda c: (0, c)),
            pl.BlockSpec((total, wide), lambda c: (0, c)),
            fixed((total, total)),
            fixed((total, total)),
            fixed((total, LABELS)),
        ),
        scratch_shapes=[
            pltpu.VMEM((total, rank), F32),
            pltpu.VMEM((total, LABELS), F32),
            pltpu.VMEM((total, ranks), F32),
        ],
        compiler_params=pltpu.CompilerParams(vmem_limit_bytes=VMEM_BYTES),
        name="project",
    )(
        arrived,
        cache,
        cache,
        cache,
        filter_tap_weight,
        filter_bias.reshape(1, chans),
        lowrank_step_weight,
        maps_weight,
        adapter_down_maps,
    )

    arrived_gate, normed, tail = pl.pallas_call(
        functools.partial(join, owners, per_owner, steps, tp_count),
        out_shape=(
            shape((owners, block, chans), BF16),
            shape((tp_count, share, rank), BF16),
            shape((tp_count, share, LABELS), F32),
        ),
        in_specs=[whole_vmem()] * 6,
        out_specs=(whole_any(), whole_any(), whole_any()),
        scratch_shapes=[
            pltpu.VMEM((owners, block, chans), BF16),
            pltpu.VMEM((tp_count - 1, share, rank + LABELS), BF16),
            pltpu.VMEM((share, rank), BF16),
            pltpu.VMEM((share, LABELS), F32),
            dma((owners,)),
            dma((owners,)),
            dma,
            dma((tp_count,)),
            dma((tp_count,)),
            dma((tp_count,)),
            dma((tp_count,)),
            dma((tp_count,)),
            dma((tp_count,)),
            dma((2,)),
        ],
        compiler_params=pltpu.CompilerParams(
            collective_id=1, has_side_effects=True, vmem_limit_bytes=VMEM_BYTES
        ),
        name="join",
    )(
        holder,
        gate,
        part,
        mask.reshape(tp_count, share, LABELS),
        adapter_up_maps,
        step_size_gain.reshape(1, rank),
    )

    new_cache, result = pl.pallas_call(
        functools.partial(scan, steps),
        grid=(chans // wide,),
        out_shape=(
            shape((depth, slots, chans), BF16),
            shape((owners, block, chans), BF16),
        ),
        in_specs=[
            fixed((total, rank)),
            fixed((total, LABELS)),
            pl.BlockSpec((rank, wide), lambda c: (0, c)),
            pl.BlockSpec((1, wide), lambda c: (0, c)),
            pl.BlockSpec((STATE, wide), lambda c: (0, c)),
            pl.BlockSpec((1, wide), lambda c: (0, c)),
            pl.BlockSpec((total, wide), lambda c: (0, c)),
            pl.BlockSpec((total, wide), lambda c: (0, c)),
            whole_vmem(),
            fixed((total, total)),
            fixed((total, total)),
            pl.BlockSpec((depth, slots, wide), lambda c: (0, 0, c)),
        ],
        out_specs=(
            pl.BlockSpec((depth, slots, wide), lambda c: (0, 0, c)),
            pl.BlockSpec((owners, block, wide), lambda c: (0, 0, c)),
        ),
        scratch_shapes=[
            pltpu.VMEM((2 * STATE, total, LABELS), F32),
            pltpu.VMEM((total, wide), F32),
            pltpu.VMEM((total, wide), F32),
            pltpu.VMEM((total, wide), F32),
            pltpu.VMEM((slots, LABELS), F32),
            pltpu.VMEM((STATE, wide), F32),
        ],
        compiler_params=pltpu.CompilerParams(vmem_limit_bytes=VMEM_BYTES),
        name="scan",
    )(
        normed.reshape(total, rank),
        tail.reshape(total, LABELS),
        step_up_weight,
        step_size_bias.reshape(1, chans),
        log_decay_rates,
        skip_factor.reshape(1, chans),
        act,
        by_slot,
        arrived_gate,
        to_arrival,
        to_slot,
        cache,
    )

    gated = pl.pallas_call(
        functools.partial(return_rows, owners),
        out_shape=shape((lanes, chans), BF16),
        in_specs=[whole_vmem()] * 2,
        out_specs=whole_vmem(),
        scratch_shapes=[
            pltpu.VMEM((owners, block, chans), BF16),
            dma((owners,)),
            dma((owners,)),
            dma,
        ],
        compiler_params=pltpu.CompilerParams(
            collective_id=2, has_side_effects=True, vmem_limit_bytes=VMEM_BYTES
        ),
        name="return_rows",
    )(back, result)
    return (gated.reshape(served, steps, chans), jnp.swapaxes(new_cache, 0, 1))


def solution(mesh):
    placed = (
        P("pool", None, "tp"),
        P("pool", None, "tp"),
        P("pool", None, "tp"),
        P("pool"),
        P("pool"),
        P("pool"),
        P(None, "tp"),
        P("tp"),
        P("tp", None),
        P("tp", None),
        P("tp", None),
        P(),
        P(),
        P(None, "tp"),
        P("tp"),
        P(None, "tp"),
        P("tp"),
    )
    return jax.shard_map(
        local,
        mesh=mesh,
        in_specs=placed,
        out_specs=(P("pool", None, "tp"), P("pool", None, "tp")),
        check_vma=False,
    )
```

```python
import functools

import jax
import jax.numpy as jnp
from jax import lax
from jax.experimental import pallas as pl
from jax.experimental.pallas import tpu as pltpu
from jax.sharding import PartitionSpec as P

STATE = 16
ADAPTER_RANK = 16
TENANT_COUNT = 64
LABELS = 128
MIB = 1024 * 1024
LOG2_E = 1.4426950408889634
F32 = jnp.float32
BF16 = jnp.bfloat16


def iota(shape, dim):
    return lax.broadcasted_iota(jnp.int32, shape, dim)


def as_bf16(mask):
    return jnp.where(mask, 1.0, 0.0).astype(BF16)


def whole_vmem():
    return pl.BlockSpec(memory_space=pltpu.VMEM)


def whole_any():
    return pl.BlockSpec(memory_space=pl.ANY)


def fixed(shape):
    return pl.BlockSpec(shape, lambda c: (0,) * len(shape))


def per_lane(numbers, steps):
    rows = numbers.shape[1]
    shape = (rows, rows * steps)
    wide = as_bf16(iota(shape, 0) == iota(shape, 1) // steps)
    return jnp.dot(numbers.astype(F32).astype(BF16), wide, preferred_element_type=F32)


def dispatch_matrix(holder, owners, per_owner, steps):
    lanes = holder.shape[1] * steps
    holder = per_lane(holder, steps)
    named = jnp.where(iota((owners, lanes), 0).astype(F32) == holder, 1.0, 0.0)
    earlier = as_bf16(
        (iota((lanes, lanes), 0) // steps < iota((lanes, lanes), 1) // steps)
        & (iota((lanes, lanes), 0) % steps == 0)
    )
    before = jnp.dot(named.astype(BF16), earlier, preferred_element_type=F32)
    rank = jnp.sum(named * before, axis=0, keepdims=True)
    target = holder * per_owner + rank
    shape = (owners * per_owner * steps, lanes)
    return jnp.where(
        ((iota(shape, 0) // steps).astype(F32) == target)
        & (iota(shape, 0) % steps == iota(shape, 1) % steps),
        1.0,
        0.0,
    )


def greet(pool_count, tp_count):
    announce(pool_count, tp_count)
    await_all(pool_count, tp_count)


def await_all(pool_count, tp_count):
    pl.semaphore_wait(
        pltpu.get_barrier_semaphore(), max(pool_count - 1, 0) + max(tp_count - 1, 0)
    )


def announce(pool_count, tp_count):
    barrier = pltpu.get_barrier_semaphore()
    me, mine = lax.axis_index("pool"), lax.axis_index("tp")
    for k in range(1, pool_count):
        pl.semaphore_signal(
            barrier,
            inc=1,
            device_id={"pool": lax.rem(me + k, pool_count)},
            device_id_type=pl.DeviceIdType.MESH,
        )
    for k in range(1, tp_count):
        pl.semaphore_signal(
            barrier,
            inc=1,
            device_id={"tp": lax.rem(mine + k, tp_count)},
            device_id_type=pl.DeviceIdType.MESH,
        )


def spread(source, landing, send_sem, recv_sem, local_sem, axis, count):
    me = lax.axis_index(axis)
    copies = []
    for k in range(1, count):
        there = lax.rem(me + k, count)
        copy = pltpu.make_async_remote_copy(
            src_ref=source.at[there],
            dst_ref=landing.at[me],
            send_sem=send_sem.at[k],
            recv_sem=recv_sem.at[k],
            device_id={axis: there},
            device_id_type=pl.DeviceIdType.MESH,
        )
        copy.start()
        copies.append(copy)
    own = pltpu.make_async_copy(source.at[me], landing.at[me], local_sem)
    own.start()
    copies.append(own)
    return copies


def pick_rows(selector, rows_ref, out_ref, offset=0):
    owners, block, _ = out_ref.shape
    for at in range(0, rows_ref.shape[2], 512):
        wide = min(512, rows_ref.shape[2] - at)
        rows = rows_ref[:, :, at : at + wide].astype(F32).reshape(selector.shape[1], wide)
        part = jnp.dot(selector, rows.astype(BF16), preferred_element_type=F32)
        out_ref[:, :, at : at + wide] = part.reshape(owners, block, wide).astype(BF16)


def send_rows(
    owners,
    per_owner,
    steps,
    holder_ref,
    slot_ref,
    tenant_ref,
    rows_ref,
    arrived_ref,
    back_ref,
    outgoing,
    send_sem,
    recv_sem,
    local_sem,
):
    announce(owners, 1)
    picked = dispatch_matrix(holder_ref[...], owners, per_owner, steps)
    selector = picked.astype(BF16)
    back_ref[...] = picked.T.astype(BF16)
    lanes = rows_ref.shape[0] * steps
    chans = rows_ref.shape[2]
    slots = owners * per_owner
    line = iota((LABELS, lanes), 0).astype(F32)
    labels = as_bf16(
        (line == per_lane(slot_ref[...], steps))
        | (line == per_lane(tenant_ref[...], steps) + slots)
    )
    marked = lax.dot_general(
        selector, labels, (((1,), (1,)), ((), ())), preferred_element_type=F32
    )
    outgoing[:, :, chans:] = marked.reshape(owners, per_owner * steps, LABELS).astype(BF16)
    pick_rows(selector, rows_ref, outgoing)
    await_all(owners, 1)
    for copy in spread(outgoing, arrived_ref, send_sem, recv_sem, local_sem, "pool", owners):
        copy.wait()


def project(
    steps,
    tp_count,
    arrived_ref,
    conv_ref0,
    conv_ref1,
    conv_ref2,
    tap_ref,
    bias_ref,
    low_ref,
    maps_ref,
    down_ref,
    part_ref,
    slots_ref,
    act_ref,
    to_arrival_ref,
    to_slot_ref,
    mask_ref,
    low_acc,
    maps_acc,
    down_acc,
):
    chunk = pl.program_id(0)
    slots, wide = conv_ref0.shape[1:]
    total = slots * steps
    chans = arrived_ref.shape[2] - LABELS

    @pl.when(chunk == 0)
    def _():
        labels = arrived_ref[:, :, chans:].astype(F32).reshape(total, LABELS)
        lane = iota((LABELS, total), 0)
        expand = as_bf16(lane == iota((LABELS, total), 1) % slots)
        selected = jnp.dot(labels.astype(BF16), expand, preferred_element_type=F32)
        selected = jnp.where(
            iota((total, total), 0) % steps == iota((total, total), 1) // slots, selected, 0.0
        )
        to_arrival_ref[...] = selected.astype(BF16)
        turned = selected.T.astype(BF16)
        to_slot_ref[...] = turned
        mask_ref[...] = jnp.dot(
            turned, labels.astype(BF16), preferred_element_type=F32
        ).astype(BF16)
        low_acc[...] = jnp.zeros_like(low_acc)
        maps_acc[...] = jnp.zeros_like(maps_acc)
        down_acc[...] = jnp.zeros_like(down_acc)

    columns = pl.ds(pl.multiple_of(chunk * wide, wide), wide)
    rows = arrived_ref[:, :, columns].astype(F32).reshape(total, wide).astype(BF16)
    mixed = jnp.dot(to_slot_ref[...], rows, preferred_element_type=F32)
    slots_ref[...] = mixed.astype(BF16)
    window = [conv_ref[0].astype(F32) for conv_ref in (conv_ref0, conv_ref1, conv_ref2)]
    window += [mixed[s * slots : (s + 1) * slots] for s in range(steps)]
    for s in range(steps):
        summed = jnp.broadcast_to(bias_ref[...], (slots, wide))
        for k in range(tap_ref.shape[0]):
            summed = summed + tap_ref[k : k + 1, :] * window[s + k]
        act_ref[s * slots : (s + 1) * slots, :] = (summed / (1.0 + jnp.exp(-summed))).astype(BF16)
    act = act_ref[...]
    low_acc[...] += jnp.dot(act, low_ref[...], preferred_element_type=F32)
    maps_acc[:, : 2 * STATE] += lax.dot_general(
        act, maps_ref[...], (((1,), (1,)), ((), ())), preferred_element_type=F32
    )
    down_acc[...] += jnp.dot(act, down_ref[...], preferred_element_type=F32)

    @pl.when(chunk == pl.num_programs(0) - 1)
    def _():
        ranks = down_acc.shape[1]
        column = iota((LABELS, ranks), 1) // ADAPTER_RANK
        keep = jnp.dot(
            mask_ref[...],
            as_bf16(iota((LABELS, ranks), 0) == column + slots),
            preferred_element_type=F32,
        )
        chosen = down_acc[...] * keep
        folded = chosen[:, :LABELS]
        for at in range(LABELS, ranks, LABELS):
            folded = folded + chosen[:, at : at + LABELS]
        fold = as_bf16(
            iota((LABELS, LABELS), 1)
            == iota((LABELS, LABELS), 0) % ADAPTER_RANK + 2 * STATE
        )
        tail = maps_acc[...] + jnp.dot(folded.astype(BF16), fold, preferred_element_type=F32)
        rank = low_acc.shape[1]
        part_ref[:, :, :rank] = (
            low_acc[...].reshape(tp_count, total // tp_count, rank).astype(BF16)
        )
        part_ref[:, :, rank:] = tail.reshape(tp_count, total // tp_count, LABELS).astype(BF16)


def join(
    owners,
    per_owner,
    steps,
    tp_count,
    holder_ref,
    gate_ref,
    part_ref,
    mask_ref,
    up_ref,
    gain_ref,
    arrived_ref,
    normed_ref,
    tail_ref,
    outgoing,
    landed,
    normed_own,
    tail_own,
    gate_send,
    gate_recv,
    gate_local,
    part_send,
    part_recv,
    normed_send,
    normed_recv,
    tail_send,
    tail_recv,
    own_sem,
):
    mine = lax.axis_index("tp")
    greet(owners, tp_count)
    first = []
    for k in range(1, tp_count):
        there = lax.rem(mine + k, tp_count)
        copy = pltpu.make_async_remote_copy(
            src_ref=part_ref.at[there],
            dst_ref=landed.at[k - 1],
            send_sem=part_send.at[k],
            recv_sem=part_recv.at[k],
            device_id={"tp": there},
            device_id_type=pl.DeviceIdType.MESH,
        )
        copy.start()
        first.append(copy)
    selector = dispatch_matrix(holder_ref[...], owners, per_owner, steps).astype(BF16)
    pick_rows(selector, gate_ref, outgoing)
    gates = spread(outgoing, arrived_ref, gate_send, gate_recv, gate_local, "pool", owners)
    summed = part_ref[mine].astype(F32)
    for k in range(1, tp_count):
        first[k - 1].wait()
        summed = summed + landed[k - 1].astype(F32)
    rank = gain_ref.shape[1]
    low, tail = summed[:, :rank], summed[:, rank:]
    ranks = up_ref.shape[0]
    slots = owners * per_owner
    column = iota((LABELS, ranks), 1)
    lane = iota((LABELS, ranks), 0)
    repeated = jnp.dot(
        tail.astype(BF16),
        as_bf16(lane == column % ADAPTER_RANK + 2 * STATE),
        preferred_element_type=F32,
    )
    keep = jnp.dot(
        mask_ref[mine],
        as_bf16(lane == column // ADAPTER_RANK + slots),
        preferred_element_type=F32,
    )
    middle = (repeated * keep).astype(BF16)
    pre = low + jnp.dot(middle, up_ref[...], preferred_element_type=F32)
    mean_sq = jnp.mean(pre * pre, axis=1, keepdims=True)
    normed_own[...] = (pre / jnp.sqrt(mean_sq + 1e-06) * gain_ref[...]).astype(BF16)
    tail_own[...] = tail
    last = []
    for number, (own, landing, send_sem, recv_sem) in enumerate(
        (
            (normed_own, normed_ref, normed_send, normed_recv),
            (tail_own, tail_ref, tail_send, tail_recv),
        )
    ):
        for k in range(1, tp_count):
            copy = pltpu.make_async_remote_copy(
                src_ref=own,
                dst_ref=landing.at[mine],
                send_sem=send_sem.at[k],
                recv_sem=recv_sem.at[k],
                device_id={"tp": lax.rem(mine + k, tp_count)},
                device_id_type=pl.DeviceIdType.MESH,
            )
            copy.start()
            last.append(copy)
        kept = pltpu.make_async_copy(own, landing.at[mine], own_sem.at[number])
        kept.start()
        last.append(kept)
    for copy in last + gates:
        copy.wait()


def scan(
    steps,
    normed_ref,
    tail_ref,
    up_ref,
    bias_ref,
    rate_ref,
    skip_ref,
    act_ref,
    slots_ref,
    gate_ref,
    to_arrival_ref,
    to_slot_ref,
    cache_ref,
    new_ref,
    out_ref,
    maps,
    delta,
    driven,
    result,
    reached,
    decay,
):
    slots, wide = cache_ref.shape[1:]
    total = slots * steps
    group, tile = 16, LABELS
    tiles = wide // tile
    chunk = pl.program_id(0)

    @pl.when(chunk == 0)
    def _():
        for n in range(2 * STATE):
            maps[n] = jnp.broadcast_to(tail_ref[:, n : n + 1], (total, LABELS))
        found = jnp.sum(to_slot_ref[:slots, :].astype(F32), axis=1, keepdims=True)
        reached[...] = jnp.broadcast_to(found, (slots, LABELS))

    drawn = jnp.dot(normed_ref[...], up_ref[...], preferred_element_type=F32) + bias_ref[...]
    size = jnp.maximum(drawn, 0.0) + jnp.log1p(jnp.exp(-jnp.abs(drawn)))
    act = act_ref[...].astype(F32)
    delta[...] = size
    driven[...] = size * act
    decay[...] = jnp.exp(rate_ref[...]) * -LOG2_E

    def one(place, carry):
        first = place // tiles * group
        rows = pl.ds(pl.multiple_of(first, group), group)
        cols = pl.ds(pl.multiple_of(lax.rem(place, tiles) * tile, tile), tile)
        at = [pl.ds(pl.multiple_of(s * slots + first, group), group) for s in range(steps)]
        sizes = [delta[at[s], cols] for s in range(steps)]
        pushes = [driven[at[s], cols] for s in range(steps)]
        served = reached[rows, :] > 0.5
        sums = [jnp.zeros((group, tile), F32)] * steps
        for n in range(STATE):
            old = cache_ref[n, rows, cols].astype(F32)
            base = decay[n : n + 1, cols]
            state = old
            for s in range(steps):
                state = jnp.exp2(sizes[s] * base) * state + pushes[s] * maps[n, at[s], :]
                sums[s] = sums[s] + maps[STATE + n, at[s], :] * state
            new_ref[n, rows, cols] = jnp.where(served, state, old).astype(BF16)
        for s in range(steps):
            result[at[s], cols] = sums[s]
        kept = cache_ref.shape[0] - STATE
        for k in range(kept):
            taken = slots_ref[at[steps - kept + k], cols].astype(F32)
            old = cache_ref[STATE + k, rows, cols].astype(F32)
            new_ref[STATE + k, rows, cols] = jnp.where(served, taken, old).astype(BF16)
        return carry

    lax.fori_loop(0, slots // group * tiles, one, 0)
    columns = pl.ds(pl.multiple_of(chunk * wide, wide), wide)
    rows = gate_ref[:, :, columns].astype(F32).reshape(total, wide).astype(BF16)
    gate = jnp.dot(to_slot_ref[...], rows, preferred_element_type=F32)
    gated = (result[...] + skip_ref[...] * act) * (gate / (1.0 + jnp.exp(-gate)))
    back = jnp.dot(to_arrival_ref[...], gated.astype(BF16), preferred_element_type=F32)
    out_ref[...] = back.reshape(out_ref.shape).astype(BF16)


def return_rows(owners, back_ref, result_ref, out_ref, landed, send_sem, recv_sem, local_sem):
    greet(owners, 1)
    for copy in spread(result_ref, landed, send_sem, recv_sem, local_sem, "pool", owners):
        copy.wait()
    total = back_ref.shape[1]
    for at in range(0, out_ref.shape[2], 512):
        rows = landed[:, :, at : at + 512].astype(F32).reshape(total, 512).astype(BF16)
        part = jnp.dot(back_ref[...], rows, preferred_element_type=F32)
        out_ref[:, :, at : at + 512] = part.reshape(out_ref.shape[:2] + (512,)).astype(BF16)


def local(
    projected_mixer,
    projected_gate,
    slot_state_cache,
    session_holder,
    session_slot,
    conversation_customer,
    filter_tap_weight,
    filter_bias,
    lowrank_step_weight,
    state_maps_weight,
    adapter_down_maps,
    adapter_up_maps,
    step_size_gain,
    step_up_weight,
    step_size_bias,
    log_decay_rates,
    skip_factor,
):
    owners, tp_count = lax.axis_size("pool"), lax.axis_size("tp")
    slots, depth, chans = slot_state_cache.shape
    served, steps, _ = projected_mixer.shape
    per_owner = slots // owners
    block = per_owner * steps
    total = slots * steps
    share = total // tp_count
    lanes = served * steps
    rank = lowrank_step_weight.shape[1]
    ranks = adapter_down_maps.shape[1]
    dma = pltpu.SemaphoreType.DMA
    shape = jax.ShapeDtypeStruct

    holder = session_holder.reshape(1, served)
    slot = session_slot.reshape(1, served)
    tenant = conversation_customer.reshape(1, served)
    cache = jnp.swapaxes(slot_state_cache, 0, 1)
    maps_weight = state_maps_weight.T

    def conv_row(k):
        return pl.BlockSpec((1, slots, wide), lambda c: (k, 0, c))

    arrived, back = pl.pallas_call(
        functools.partial(send_rows, owners, per_owner, steps),
        out_shape=(
            shape((owners, block, chans + LABELS), BF16),
            shape((lanes, total), BF16),
        ),
        in_specs=[whole_vmem()] * 4,
        out_specs=(whole_any(), whole_vmem()),
        scratch_shapes=[
            pltpu.VMEM((owners, block, chans + LABELS), BF16),
            dma((owners,)),
            dma((owners,)),
            dma,
        ],
        compiler_params=pltpu.CompilerParams(
            collective_id=0, has_side_effects=True, vmem_limit_bytes=10 * MIB
        ),
        cost_estimate=pl.CostEstimate(flops=0, bytes_accessed=60 * MIB, transcendentals=0),
        name="send_rows",
    )(holder, slot, tenant, projected_mixer)

    wide = min(512, chans)
    part, by_slot, act, to_arrival, to_slot, mask = pl.pallas_call(
        functools.partial(project, steps, tp_count),
        grid=(chans // wide,),
        out_shape=(
            shape((tp_count, share, rank + LABELS), BF16),
            shape((total, chans), BF16),
            shape((total, chans), BF16),
            shape((total, total), BF16),
            shape((total, total), BF16),
            shape((total, LABELS), BF16),
        ),
        in_specs=[
            whole_vmem(),
            conv_row(depth - 3),
            conv_row(depth - 2),
            conv_row(depth - 1),
            pl.BlockSpec((filter_tap_weight.shape[0], wide), lambda c: (0, c)),
            pl.BlockSpec((1, wide), lambda c: (0, c)),
            pl.BlockSpec((wide, rank), lambda c: (c, 0)),
            pl.BlockSpec((2 * STATE, wide), lambda c: (0, c)),
            pl.BlockSpec((wide, ranks), lambda c: (c, 0)),
        ],
        out_specs=(
            fixed((tp_count, share, rank + LABELS)),
            pl.BlockSpec((total, wide), lambda c: (0, c)),
            pl.BlockSpec((total, wide), lambda c: (0, c)),
            fixed((total, total)),
            fixed((total, total)),
            fixed((total, LABELS)),
        ),
        scratch_shapes=[
            pltpu.VMEM((total, rank), F32),
            pltpu.VMEM((total, LABELS), F32),
            pltpu.VMEM((total, ranks), F32),
        ],
        compiler_params=pltpu.CompilerParams(vmem_limit_bytes=50 * MIB),
        cost_estimate=pl.CostEstimate(flops=0, bytes_accessed=26 * MIB, transcendentals=0),
        name="project",
    )(
        arrived,
        cache,
        cache,
        cache,
        filter_tap_weight,
        filter_bias.reshape(1, chans),
        lowrank_step_weight,
        maps_weight,
        adapter_down_maps,
    )

    arrived_gate, normed, tail = pl.pallas_call(
        functools.partial(join, owners, per_owner, steps, tp_count),
        out_shape=(
            shape((owners, block, chans), BF16),
            shape((tp_count, share, rank), BF16),
            shape((tp_count, share, LABELS), F32),
        ),
        in_specs=[whole_vmem()] * 6,
        out_specs=(whole_any(), whole_any(), whole_any()),
        scratch_shapes=[
            pltpu.VMEM((owners, block, chans), BF16),
            pltpu.VMEM((tp_count - 1, share, rank + LABELS), BF16),
            pltpu.VMEM((share, rank), BF16),
            pltpu.VMEM((share, LABELS), F32),
            dma((owners,)),
            dma((owners,)),
            dma,
            dma((tp_count,)),
            dma((tp_count,)),
            dma((tp_count,)),
            dma((tp_count,)),
            dma((tp_count,)),
            dma((tp_count,)),
            dma((2,)),
        ],
        compiler_params=pltpu.CompilerParams(
            collective_id=1, has_side_effects=True, vmem_limit_bytes=14 * MIB
        ),
        cost_estimate=pl.CostEstimate(flops=0, bytes_accessed=74 * MIB, transcendentals=0),
        name="join",
    )(
        holder,
        projected_gate,
        part,
        mask.reshape(tp_count, share, LABELS),
        adapter_up_maps,
        step_size_gain.reshape(1, rank),
    )

    new_cache, result = pl.pallas_call(
        functools.partial(scan, steps),
        grid=(chans // wide,),
        out_shape=(
            shape((depth, slots, chans), BF16),
            shape((owners, block, chans), BF16),
        ),
        in_specs=[
            fixed((total, rank)),
            fixed((total, LABELS)),
            pl.BlockSpec((rank, wide), lambda c: (0, c)),
            pl.BlockSpec((1, wide), lambda c: (0, c)),
            pl.BlockSpec((STATE, wide), lambda c: (0, c)),
            pl.BlockSpec((1, wide), lambda c: (0, c)),
            pl.BlockSpec((total, wide), lambda c: (0, c)),
            pl.BlockSpec((total, wide), lambda c: (0, c)),
            whole_vmem(),
            fixed((total, total)),
            fixed((total, total)),
            pl.BlockSpec((depth, slots, wide), lambda c: (0, 0, c)),
        ],
        out_specs=(
            pl.BlockSpec((depth, slots, wide), lambda c: (0, 0, c)),
            pl.BlockSpec((owners, block, wide), lambda c: (0, 0, c)),
        ),
        scratch_shapes=[
            pltpu.VMEM((2 * STATE, total, LABELS), F32),
            pltpu.VMEM((total, wide), F32),
            pltpu.VMEM((total, wide), F32),
            pltpu.VMEM((total, wide), F32),
            pltpu.VMEM((slots, LABELS), F32),
            pltpu.VMEM((STATE, wide), F32),
        ],
        compiler_params=pltpu.CompilerParams(vmem_limit_bytes=36 * MIB),
        cost_estimate=pl.CostEstimate(flops=0, bytes_accessed=65 * MIB, transcendentals=0),
        name="scan",
    )(
        normed.reshape(total, rank),
        tail.reshape(total, LABELS),
        step_up_weight,
        step_size_bias.reshape(1, chans),
        log_decay_rates,
        skip_factor.reshape(1, chans),
        act,
        by_slot,
        arrived_gate,
        to_arrival,
        to_slot,
        cache,
    )

    gated = pl.pallas_call(
        functools.partial(return_rows, owners),
        out_shape=shape((served, steps, chans), BF16),
        in_specs=[whole_vmem()] * 2,
        out_specs=whole_vmem(),
        scratch_shapes=[
            pltpu.VMEM((owners, block, chans), BF16),
            dma((owners,)),
            dma((owners,)),
            dma,
        ],
        compiler_params=pltpu.CompilerParams(
            collective_id=2, has_side_effects=True, vmem_limit_bytes=8 * MIB
        ),
        cost_estimate=pl.CostEstimate(flops=0, bytes_accessed=55 * MIB, transcendentals=0),
        name="return_rows",
    )(back, result)
    return (gated, jnp.swapaxes(new_cache, 0, 1))


def solution(mesh):
    placed = (
        P("pool", None, "tp"),
        P("pool", None, "tp"),
        P("pool", None, "tp"),
        P("pool"),
        P("pool"),
        P("pool"),
        P(None, "tp"),
        P("tp"),
        P("tp", None),
        P("tp", None),
        P("tp", None),
        P(),
        P(),
        P(None, "tp"),
        P("tp"),
        P(None, "tp"),
        P("tp"),
    )
    return jax.shard_map(
        local,
        mesh=mesh,
        in_specs=placed,
        out_specs=(P("pool", None, "tp"), P("pool", None, "tp")),
        check_vma=False,
    )
```
